32 devices in a mesh: shot: 4 (over x, core), brick: 8 (over z, y).
Axes of the slice: x: 2, y: 2, z: 4, core: 2. Of those that a mesh axis runs over, the one named last changes fastest.
Arguments:
- field_prev: float32 [4, 32, 256, 256], P('shot', 'brick'), may hold values from -6 to 6
- field_now: float32 [4, 32, 256, 256], P('shot', 'brick'), may hold values from -6 to 6
- diag_coef: float32 [3, 32, 256, 256], P(None, 'brick'), may hold values from 0.06 to 0.22
- cross_coef: float32 [3, 32, 256, 256], P(None, 'brick'), may hold values from -0.08 to 0.08
- green: bfloat16 [4, 1024, 1024], P('shot', None, 'brick'), may hold values from -0.1875 to 0.1875
- delays: int32 [4], replicated, may hold values from 0 to 8
- past: bfloat16 [8, 4, 1024], P(None, 'shot', 'brick'), may hold values from -6 to 6
- rec_cell: int32 [4, 1024], P('shot', 'brick'), may hold values from 0 to 262143
- emit_cell: int32 [4, 1024], P('shot', 'brick'), may hold values from 0 to 262143
Outputs:
- field_before: float32 [4, 32, 256, 256], P('shot', 'brick')
- field_after: float32 [4, 32, 256, 256], P('shot', 'brick')
- recorded: bfloat16 [3, 4, 1024], P(None, 'shot', 'brick')
The draws below stay inside these ranges and needn't reach their ends.
Inputs may be any that keep to these rules, and one draw needn't show every extreme that they name: `rec_cell`: entries of block b (points b * 128 to (b + 1) * 128 - 1) index cells of brick b, counted within the brick. `emit_cell`: entries of block b (points b * 128 to (b + 1) * 128 - 1) index cells of brick b, counted within the brick.
All inputs are finite; a program needn't handle non-finite values.
Results may differ from the reference program's by a relative error of at most 0.001.
Values may be sent and summed in bfloat16 or wider, within the bound.
A program may use at most 64 MiB of HBM per device.

```python
import jax
import jax.numpy as jnp
from jax import lax

CX = 4
NY = 256
NZ = 256
REC_DEV = 128
EMIT_DEV = 128
HIST = 8
STEPS = 3
NX = 32
RECS = 1024
EMITS = 1024
SHOTS = 4
LAGS = 4


def set_ends(result, rng, low, largest):
    longest = result.shape.index(max(result.shape))
    spots = []
    for shift in (0, 1):
        where = [jax.random.randint(jax.random.fold_in(rng, axis), (), 0, length) for axis, length in enumerate(result.shape)]
        where[longest] = (where[longest] + shift) % result.shape[longest]
        spots.append(tuple(where))
    return result.at[spots[0]].set(low).at[spots[1]].set(largest)


def level_of(rng, dims, pieces, least, high):
    def one(dim, shards_of):
        draws = jax.random.uniform(jax.random.fold_in(jax.random.fold_in(rng, 6), dim), (shards_of,), jnp.float32, least / len(pieces), high / len(pieces))
        return jnp.repeat(jnp.exp(draws), dims[dim] // shards_of).reshape((-1,) + (1,) * (len(dims) - dim - 1))

    gain = one(*pieces[0])
    for cut in pieces[1:]:
        gain = gain * one(*cut)
    return gain


def bell_draw(rng, extent, spread, bound, pieces=(), kind=jnp.bfloat16):
    array = spread * jax.random.normal(rng, extent, jnp.float32)
    if pieces:
        array = array * level_of(rng, extent, pieces, -0.22, 0.18)
    return jnp.clip(array, -bound, bound).astype(kind)


def setup_inputs(seed: int = 0) -> dict:
    streams_of = jax.random.split(jax.random.key(seed), 10)
    return {
        "field_prev": bell_draw(streams_of[0], (SHOTS, NX, NY, NZ), 1.0, 6.0, ((0, 4), (1, 8)), jnp.float32),
        "field_now": bell_draw(streams_of[1], (SHOTS, NX, NY, NZ), 1.0, 6.0, ((0, 4), (1, 8)), jnp.float32),
        "diag_coef": jnp.clip(0.06 + 0.16 * jax.random.uniform(streams_of[2], (3, NX, NY, NZ), jnp.float32) ** level_of(streams_of[2], (3, NX, NY, NZ), ((1, 8),), -0.2, 0.2), 0.06, 0.22),
        "cross_coef": jnp.clip(jax.random.uniform(streams_of[3], (3, NX, NY, NZ), jnp.float32, -0.08, 0.08) * level_of(streams_of[3], (3, NX, NY, NZ), ((1, 8),), -0.4, 0.0), -0.08, 0.08),
        "green": bell_draw(streams_of[4], (LAGS, EMITS, RECS), RECS ** -0.5, 0.1875, ((0, 4), (2, 8))),
        "delays": set_ends(jax.random.randint(streams_of[5], (LAGS,), 0, HIST + 1), jax.random.fold_in(streams_of[5], 1), 0, HIST).astype(jnp.int32),
        "past": bell_draw(streams_of[6], (HIST, SHOTS, RECS), 1.0, 6.0, ((1, 4), (2, 8))),
        "rec_cell": set_ends(jax.random.randint(streams_of[7], (SHOTS, RECS), 0, CX * NY * NZ), jax.random.fold_in(streams_of[7], 1), 0, (CX * NY * NZ) - 1).astype(jnp.int32),
        "emit_cell": set_ends(jax.random.randint(streams_of[8], (SHOTS, EMITS), 0, CX * NY * NZ), jax.random.fold_in(streams_of[8], 1), 0, (CX * NY * NZ) - 1).astype(jnp.int32),
    }


def operate(padded, centre, diag_coef, cross_coef):
    width_x = centre.shape[1]
    width_y = centre.shape[2]
    width_z = centre.shape[3]

    def shifted(offset_x, offset_y, offset_z):
        return padded[:, 1 + offset_x:1 + offset_x + width_x, 1 + offset_y:1 + offset_y + width_y, 1 + offset_z:1 + offset_z + width_z]

    second = diag_coef[0] * (shifted(1, 0, 0) - 2.0 * centre + shifted(-1, 0, 0))
    second = second + diag_coef[1] * (shifted(0, 1, 0) - 2.0 * centre + shifted(0, -1, 0))
    second = second + diag_coef[2] * (shifted(0, 0, 1) - 2.0 * centre + shifted(0, 0, -1))
    mixed = cross_coef[0] * (shifted(1, 1, 0) - shifted(1, -1, 0) - shifted(-1, 1, 0) + shifted(-1, -1, 0))
    mixed = mixed + cross_coef[1] * (shifted(1, 0, 1) - shifted(1, 0, -1) - shifted(-1, 0, 1) + shifted(-1, 0, -1))
    mixed = mixed + cross_coef[2] * (shifted(0, 1, 1) - shifted(0, 1, -1) - shifted(0, -1, 1) + shifted(0, -1, -1))
    return second + 0.5 * mixed


def reference(field_prev, field_now, diag_coef, cross_coef, green, delays, past, rec_cell, emit_cell):
    brick_cells = CX * NY * NZ
    rec_global = ((jnp.arange(RECS) // REC_DEV) * brick_cells).astype(jnp.int32)[None, :] + rec_cell
    emit_global = ((jnp.arange(EMITS) // EMIT_DEV) * brick_cells).astype(jnp.int32)[None, :] + emit_cell
    shot_rows = jnp.arange(SHOTS).astype(jnp.int32)
    series = [past[position] for position in range(HIST)]
    earlier, current = field_prev, field_now
    recorded = []
    for moment in range(STEPS):
        flat_now = current.reshape(SHOTS, -1)
        sample = jnp.take_along_axis(flat_now, rec_global, axis=1).astype(jnp.bfloat16)
        series.append(sample)
        recorded.append(sample)
        stacked = jnp.stack(series)
        emission = jnp.zeros((SHOTS, EMITS), jnp.float32)
        for lag_index in range(LAGS):
            where_at = (HIST + moment - delays[lag_index]).astype(jnp.int32)
            chosen = lax.dynamic_index_in_dim(stacked, where_at, 0, keepdims=False)
            emission = emission + jnp.dot(chosen, green[lag_index].T, preferred_element_type=jnp.float32)
        padded = jnp.pad(current, ((0, 0), (1, 1), (1, 1), (1, 1)))
        following = 2.0 * current - earlier + operate(padded, current, diag_coef, cross_coef)
        flat_next = following.reshape(SHOTS, -1)
        flat_next = flat_next.at[shot_rows[:, None], emit_global].add(emission)
        earlier, current = current, flat_next.reshape(current.shape)
    return earlier, current, jnp.stack(recorded)
```

```python
import functools

import jax
import jax.numpy as jnp
from jax import lax
from jax.experimental import pallas as pl
from jax.experimental.pallas import tpu as pltpu
from jax.sharding import PartitionSpec as P

STEPS = 3
MESH = pl.DeviceIdType.MESH
PAD = 8
ROWS = 16
CHUNKS = 4
F32 = jnp.float32
BF16 = jnp.bfloat16


def column_of(row):
    k = row.shape[1]
    eye = lax.broadcasted_iota(jnp.int32, (k, k), 0) == lax.broadcasted_iota(jnp.int32, (k, k), 1)
    return jnp.sum(jnp.where(eye, jnp.broadcast_to(row, (k, k)), 0.0), axis=1, keepdims=True)


def row_of(col):
    k = col.shape[0]
    eye = lax.broadcasted_iota(jnp.int32, (k, k), 0) == lax.broadcasted_iota(jnp.int32, (k, k), 1)
    return jnp.sum(jnp.where(eye, jnp.broadcast_to(col, (k, k)), 0.0), axis=0, keepdims=True)


def kernel(
    n, shots, prev_hbm, now_hbm, diag_hbm, cross_hbm, green_hbm, delays, past, rec_cell, emit_cell,
    before_hbm, after_hbm, recorded,
    ua, ub, diag, cross, green, series, send_edge, recv_edge, send_sum, recv_sum,
    rec_rows, rec_lanes, emit_rows, emit_lanes, weights,
    now_sem, prev_sem, coef_sem, green_sem, green_send, green_recv, pass_send, pass_recv,
    edge_send, edge_recv, sum_send, sum_recv, out_sem,
):
    me = lax.axis_index("brick")
    shot = lax.axis_index("shot")
    cx, ny, nz = prev_hbm.shape[1:]
    hist = past.shape[0]
    points = rec_cell.shape[1]
    chunk = ny // CHUNKS
    half = shots // 2
    core = lax.rem(shot, 2)
    high = shot // 2
    peer = shot + 1 - 2 * core
    inner = pl.ds(PAD, ny)

    order = [0, cx - 1] + list(range(1, cx - 1))

    def now_copy(x):
        return pltpu.make_async_copy(now_hbm.at[0, x], ub.at[1 + x, inner], now_sem.at[x])

    def prev_copy(x):
        return pltpu.make_async_copy(prev_hbm.at[0, x], ua.at[1 + x, inner], prev_sem.at[x])

    def diag_copy(x):
        return pltpu.make_async_copy(diag_hbm.at[:, x], diag.at[:, x], coef_sem.at[0, x])

    def cross_copy(x):
        return pltpu.make_async_copy(cross_hbm.at[:, x], cross.at[:, x], coef_sem.at[1, x])

    for x in order:
        now_copy(x).start()

    barrier = pltpu.get_barrier_semaphore()
    for i in range(1, n):
        pl.semaphore_signal(
            barrier, inc=1, device_id=(shot, lax.rem(me + i, n)), device_id_type=MESH
        )
    for i in range(1, half):
        pl.semaphore_signal(
            barrier, inc=1, device_id=(lax.rem(high + i, half) * 2 + core, me), device_id_type=MESH
        )
    pl.semaphore_signal(barrier, inc=1, device_id=(peer, me), device_id_type=MESH)

    own_green = pltpu.make_async_copy(green_hbm.at[0], green.at[shot], green_sem)
    own_green.start()
    for x in order[2:] + order[:2]:
        prev_copy(x).start()
        diag_copy(x).start()
        cross_copy(x).start()

    for field in (ua, ub):
        field[0] = jnp.zeros(field.shape[1:], F32)
        field[cx + 1] = jnp.zeros(field.shape[1:], F32)
        for x in range(cx):
            field[1 + x, pl.ds(0, PAD)] = jnp.zeros((PAD, nz), F32)
            field[1 + x, pl.ds(PAD + ny, PAD)] = jnp.zeros((PAD, nz), F32)

    pl.semaphore_wait(barrier, n - 1 + half)

    def green_copy(i):
        return pltpu.make_async_remote_copy(
            src_ref=green_hbm.at[0],
            dst_ref=green.at[shot],
            send_sem=green_send.at[i],
            recv_sem=green_recv.at[i],
            device_id=(lax.rem(high + i, half) * 2 + core, me) if i else (peer, me),
            device_id_type=MESH,
        )

    def green_wait(i):
        source = lax.rem(high - i + half, half) * 2 + core if i else peer
        pltpu.make_async_remote_copy(
            src_ref=green_hbm.at[0],
            dst_ref=green.at[source],
            send_sem=green_send.at[i],
            recv_sem=green_recv.at[i],
            device_id=(peer, me),
            device_id_type=MESH,
        ).wait_recv()

    def pass_copy(i, which):
        slot = lax.rem(high - i + half, half) * 2 + which
        return pltpu.make_async_remote_copy(
            src_ref=green.at[slot],
            dst_ref=green.at[slot],
            send_sem=pass_send.at[i],
            recv_sem=pass_recv.at[i],
            device_id=(peer, me),
            device_id_type=MESH,
        )

    for i in list(range(1, half)) + [0]:
        green_copy(i).start()

    def edge_copy(t, side, k):
        rows = pl.ds(k * chunk, chunk)
        return pltpu.make_async_remote_copy(
            src_ref=send_edge.at[t, side, rows],
            dst_ref=recv_edge.at[t, side, rows],
            send_sem=edge_send.at[t, side, k],
            recv_sem=edge_recv.at[t, side, k],
            device_id=(shot, lax.rem(me + 1 - 2 * side + n, n)),
            device_id_type=MESH,
        )

    def sends_to(side):
        return me < n - 1 if side == 0 else me > 0

    def hears_from(side):
        return me > 0 if side == 0 else me < n - 1

    def send_edges(field, t, k):
        for side in (0, 1):
            plane = cx if side == 0 else 1
            send_edge[t, side, pl.ds(k * chunk, chunk)] = field[
                plane, pl.ds(PAD + k * chunk, chunk)
            ].astype(BF16)

            @pl.when(sends_to(side))
            def _():
                edge_copy(t, side, k).start()

    def take_edges(field, t, k):
        for side in (0, 1):
            plane = 0 if side == 0 else cx + 1

            @pl.when(hears_from(side))
            def _():
                edge_copy(t, side, k).wait_recv()
                field[plane, pl.ds(PAD + k * chunk, chunk)] = recv_edge[
                    t, side, pl.ds(k * chunk, chunk)
                ].astype(F32)

    now_copy(0).wait()
    now_copy(cx - 1).wait()
    for k in range(CHUNKS):
        send_edges(ub, 0, k)

    cells = rec_cell[...]
    row_col = column_of((cells // nz).astype(F32))
    lane_col = column_of((cells % nz).astype(F32))
    rec_rows[...] = jnp.where(
        lax.broadcasted_iota(jnp.int32, (points, cx * ny), 1).astype(F32) == row_col, 1.0, 0.0
    ).astype(BF16)
    lanes = lax.broadcasted_iota(jnp.int32, (points, nz), 1).astype(F32)
    rec_lanes[...] = jnp.where(lanes == lane_col, 1.0, 0.0)
    cells = emit_cell[...]
    hits = jnp.where(
        lax.broadcasted_iota(jnp.int32, (cx * ny, points), 0) == cells // nz, 1.0, 0.0
    ).astype(BF16)
    emit_rows[:, pl.ds(0, points)] = hits
    emit_rows[:, pl.ds(points, points)] = hits
    emit_lanes[...] = jnp.where(lanes == column_of((cells % nz).astype(F32)), 1.0, 0.0)
    series[...] = jnp.zeros(series.shape, F32)
    series[pl.ds(0, hist), :] = past[...]

    def record(field, t):
        picked = jnp.zeros((points, nz), F32)
        for x in range(cx):
            picked = picked + jnp.dot(
                rec_rows[:, pl.ds(x * ny, ny)],
                field[1 + x, inner].astype(BF16),
                preferred_element_type=F32,
            )
        sample = row_of(jnp.sum(picked * rec_lanes[...], axis=1, keepdims=True))
        recorded[pl.ds(t, 1), :] = sample
        series[pl.ds(hist + t, 1), :] = sample

    def sum_copy(t, i):
        to = lax.rem(me + i, n)
        return pltpu.make_async_remote_copy(
            src_ref=send_sum.at[t, to],
            dst_ref=recv_sum.at[t, me],
            send_sem=sum_send.at[t, i - 1],
            recv_sem=sum_recv.at[t, i - 1],
            device_id=(shot, to),
            device_id_type=MESH,
        )

    def sum_wait(t, i):
        pltpu.make_async_remote_copy(
            src_ref=send_sum.at[t, lax.rem(me + i, n)],
            dst_ref=recv_sum.at[t, lax.rem(me - i + n, n)],
            send_sem=sum_send.at[t, i - 1],
            recv_sem=sum_recv.at[t, i - 1],
            device_id=(shot, lax.rem(me + i, n)),
            device_id_type=MESH,
        ).wait_recv()

    def emit_start(t):
        total = None
        steps_of = lax.broadcasted_iota(jnp.int32, series.shape, 0)
        for lag in range(shots):
            where_at = hist + t - delays[lag]
            chosen = jnp.sum(jnp.where(steps_of == where_at, series[...], 0.0), axis=0, keepdims=True)
            part = lax.dot_general(
                jnp.broadcast_to(chosen, (16, points)).astype(BF16),
                green[lag],
                (((1,), (1,)), ((), ())),
                preferred_element_type=F32,
            )
            total = part if total is None else total + part
        for k in range(n):
            send_sum[t, k] = total[0:1, k * points:(k + 1) * points]
        for i in range(1, n):
            sum_copy(t, i).start()
        recv_sum[t, me] = send_sum[t, me]

    def emit_finish(t):
        for i in range(1, n):
            sum_wait(t, i)
        total = recv_sum[t, 0]
        for k in range(1, n):
            total = total + recv_sum[t, k]
        spread = emit_lanes[...] * column_of(total)
        upper = spread.astype(BF16)
        weights[pl.ds(0, points), :] = upper
        weights[pl.ds(points, points), :] = (spread - upper.astype(F32)).astype(BF16)

    def add_emission(field, x, start, rows):
        field[1 + x, pl.ds(PAD + start, rows)] += jnp.dot(
            emit_rows[pl.ds(x * ny + start, rows), :], weights[...], preferred_element_type=F32
        )

    lane = lax.broadcasted_iota(jnp.int32, (ROWS, nz), 1)
    not_first = lane > 0
    not_last = lane < nz - 1

    def ahead(v):
        return jnp.where(not_last, pltpu.roll(v, nz - 1, 1), 0.0)

    def behind(v):
        return jnp.where(not_first, pltpu.roll(v, 1, 1), 0.0)

    def later(slab):
        return pltpu.roll(slab, ROWS + 2 * PAD - 1, 0)[PAD:PAD + ROWS]

    def sooner(slab):
        return pltpu.roll(slab, 1, 0)[PAD:PAD + ROWS]

    def advance(earlier, current, x, start, rows):
        def body(i, _):
            y = pl.multiple_of(start + i * ROWS, ROWS)
            here = pl.ds(pl.multiple_of(y + PAD, PAD), ROWS)
            around = pl.ds(y, ROWS + 2 * PAD)
            at = pl.ds(y, ROWS)
            centre = current[1 + x, around]
            difference = current[2 + x, around] - current[x, around]
            u = current[1 + x, here]
            above, below = current[2 + x, here], current[x, here]
            u_up, u_down = later(centre), sooner(centre)
            twice = 2.0 * u
            second = diag[0, x, at] * (above + below - twice)
            second = second + diag[1, x, at] * (u_up + u_down - twice)
            second = second + diag[2, x, at] * (ahead(u) + behind(u) - twice)
            across = above - below
            slope = u_up - u_down
            mixed = cross[0, x, at] * (
                later(difference) - sooner(difference)
            )
            mixed = mixed + cross[1, x, at] * (ahead(across) - behind(across))
            mixed = mixed + cross[2, x, at] * (ahead(slope) - behind(slope))
            earlier[1 + x, here] = twice - earlier[1 + x, here] + second + 0.5 * mixed
            return 0

        lax.fori_loop(0, rows // ROWS, body, 0)

    for x in range(1, cx - 1):
        now_copy(x).wait()

    for t in range(STEPS):
        earlier, current = (ua, ub) if t % 2 == 0 else (ub, ua)
        record(current, t)
        if t > 0:
            emit_start(t)
        for x in range(1, cx - 1):
            if t == 0:
                prev_copy(x).wait()
                diag_copy(x).wait()
                cross_copy(x).wait()
            advance(earlier, current, x, 0, ny)
        if t == 0:
            for i in range(1, half):
                green_wait(i)
                pass_copy(i, core).start()
            own_green.wait()
            green_wait(0)
            for i in range(1, half):
                pass_copy(i, 1 - core).wait_recv()
            emit_start(t)
            for x in (0, cx - 1):
                prev_copy(x).wait()
                diag_copy(x).wait()
                cross_copy(x).wait()
        emit_finish(t)
        for x in range(1, cx - 1):
            add_emission(earlier, x, 0, ny)
        take_edges(current, t, 0)
        for k in range(CHUNKS):
            if k + 1 < CHUNKS:
                take_edges(current, t, k + 1)
            for x in (0, cx - 1):
                advance(earlier, current, x, k * chunk, chunk)
                add_emission(earlier, x, k * chunk, chunk)
            if t + 1 < STEPS:
                send_edges(earlier, t + 1, k)
        if t == STEPS - 2:
            before = pltpu.make_async_copy(
                earlier.at[pl.ds(1, cx), inner], before_hbm.at[0], out_sem.at[0]
            )
            before.start()
        if t == STEPS - 1:
            after = pltpu.make_async_copy(
                earlier.at[pl.ds(1, cx), inner], after_hbm.at[0], out_sem.at[1]
            )
            after.start()

    for i in range(half):
        green_copy(i).wait_send()
    for i in range(1, half):
        pass_copy(i, core).wait_send()
    for t in range(STEPS):
        for i in range(1, n):
            sum_copy(t, i).wait_send()
        for side in (0, 1):

            @pl.when(sends_to(side))
            def _():
                for k in range(CHUNKS):
                    edge_copy(t, side, k).wait_send()

    before.wait()
    after.wait()


def on_device(
    n, shots, field_prev, field_now, diag_coef, cross_coef, green, delays, past, rec_cell, emit_cell
):
    _, cx, ny, nz = field_prev.shape
    hist, _, points = past.shape
    _, emits, _ = green.shape
    half = shots // 2
    vmem = pl.BlockSpec(memory_space=pltpu.VMEM)
    hbm = pl.BlockSpec(memory_space=pl.ANY)
    dma = pltpu.SemaphoreType.DMA
    depth = -(-(hist + STEPS) // 8) * 8
    before, after, recorded = pl.pallas_call(
        functools.partial(kernel, n, shots),
        out_shape=(
            jax.ShapeDtypeStruct(field_prev.shape, F32),
            jax.ShapeDtypeStruct(field_prev.shape, F32),
            jax.ShapeDtypeStruct((STEPS, points), F32),
        ),
        in_specs=[hbm] * 5 + [pl.BlockSpec(memory_space=pltpu.SMEM)] + [vmem] * 3,
        out_specs=(hbm, hbm, vmem),
        scratch_shapes=[
            pltpu.VMEM((cx + 2, ny + 2 * PAD, nz), F32),
            pltpu.VMEM((cx + 2, ny + 2 * PAD, nz), F32),
            pltpu.VMEM((3, cx, ny, nz), F32),
            pltpu.VMEM((3, cx, ny, nz), F32),
            pltpu.VMEM((shots, emits, points), BF16),
            pltpu.VMEM((depth, points), F32),
            pltpu.VMEM((STEPS, 2, ny, nz), BF16),
            pltpu.VMEM((STEPS, 2, ny, nz), BF16),
            pltpu.VMEM((STEPS, n, 1, points), F32),
            pltpu.VMEM((STEPS, n, 1, points), F32),
            pltpu.VMEM((points, cx * ny), BF16),
            pltpu.VMEM((points, nz), F32),
            pltpu.VMEM((cx * ny, 2 * points), BF16),
            pltpu.VMEM((points, nz), F32),
            pltpu.VMEM((2 * points, nz), BF16),
            dma((cx,)),
            dma((cx,)),
            dma((2, cx)),
            dma,
            dma((half,)),
            dma((half,)),
            dma((half,)),
            dma((half,)),
            dma((STEPS, 2, CHUNKS)),
            dma((STEPS, 2, CHUNKS)),
            dma((STEPS, n - 1)),
            dma((STEPS, n - 1)),
            dma((2,)),
        ],
        compiler_params=pltpu.CompilerParams(
            collective_id=0, has_side_effects=True, vmem_limit_bytes=48 * 1024 * 1024
        ),
    )(
        field_prev,
        field_now,
        diag_coef,
        cross_coef,
        green,
        delays,
        past.reshape(hist, points).astype(F32),
        rec_cell,
        emit_cell,
    )
    return before, after, recorded.astype(BF16).reshape(STEPS, 1, points)


def solution(mesh):
    return jax.shard_map(
        functools.partial(on_device, mesh.shape["brick"], mesh.shape["shot"]),
        mesh=mesh,
        in_specs=(
            P("shot", "brick", None, None),
            P("shot", "brick", None, None),
            P(None, "brick", None, None),
            P(None, "brick", None, None),
            P("shot", None, "brick"),
            P(),
            P(None, "shot", "brick"),
            P("shot", "brick"),
            P("shot", "brick"),
        ),
        out_specs=(
            P("shot", "brick", None, None),
            P("shot", "brick", None, None),
            P(None, "shot", "brick"),
        ),
        check_vma=False,
    )
```

```python
import functools

import jax
import jax.numpy as jnp
from jax import lax
from jax.experimental import pallas as pl
from jax.experimental.pallas import tpu as pltpu
from jax.sharding import PartitionSpec as P

STEPS = 3
MESH = pl.DeviceIdType.MESH
PAD = 8
ROWS = 32
CHUNKS = 4
F32 = jnp.float32
BF16 = jnp.bfloat16


def column_of(row):
    k = row.shape[1]
    eye = lax.broadcasted_iota(jnp.int32, (k, k), 0) == lax.broadcasted_iota(jnp.int32, (k, k), 1)
    return jnp.sum(jnp.where(eye, jnp.broadcast_to(row, (k, k)), 0.0), axis=1, keepdims=True)


def row_of(col):
    k = col.shape[0]
    eye = lax.broadcasted_iota(jnp.int32, (k, k), 0) == lax.broadcasted_iota(jnp.int32, (k, k), 1)
    return jnp.sum(jnp.where(eye, jnp.broadcast_to(col, (k, k)), 0.0), axis=0, keepdims=True)


def kernel(
    n, shots, prev_hbm, now_hbm, diag_hbm, cross_hbm, green_hbm, delays, past_hbm, rec_hbm, emit_hbm,
    before_hbm, after_hbm, recorded,
    past, rec_cell, emit_cell, ua, ub, diag, cross, green, series, send_edge, recv_edge, send_sum, recv_sum,
    rec_rows, rec_lanes, emit_rows, emit_lanes, weights,
    small_sem, now_sem, prev_sem, coef_sem, green_sem, green_send, green_recv, pass_send, pass_recv,
    edge_send, edge_recv, sum_send, sum_recv, out_sem,
):
    me = lax.axis_index("brick")
    shot = lax.axis_index("shot")
    cx, ny, nz = prev_hbm.shape[1:]
    hist = past.shape[0]
    points = rec_cell.shape[1]
    chunk = ny // CHUNKS
    half = shots // 2
    core = lax.rem(shot, 2)
    high = shot // 2
    peer = shot + 1 - 2 * core
    inner = pl.ds(PAD, ny)

    order = [0, cx - 1] + list(range(1, cx - 1))

    def now_copy(x):
        return pltpu.make_async_copy(now_hbm.at[0, x], ub.at[1 + x, inner], now_sem.at[x])

    def prev_copy(x):
        return pltpu.make_async_copy(prev_hbm.at[0, x], ua.at[1 + x, inner], prev_sem.at[x])

    def diag_copy(x):
        return pltpu.make_async_copy(diag_hbm.at[:, x], diag.at[:, x], coef_sem.at[0, x])

    def cross_copy(x):
        return pltpu.make_async_copy(cross_hbm.at[:, x], cross.at[:, x], coef_sem.at[1, x])

    for x in order:
        now_copy(x).start()
    small = [
        pltpu.make_async_copy(source, target, small_sem.at[i])
        for i, (source, target) in enumerate(
            ((past_hbm, past), (rec_hbm, rec_cell), (emit_hbm, emit_cell))
        )
    ]
    for copy in small:
        copy.start()

    barrier = pltpu.get_barrier_semaphore()
    for i in range(1, n):
        pl.semaphore_signal(
            barrier, inc=1, device_id=(shot, lax.rem(me + i, n)), device_id_type=MESH
        )
    for i in range(1, half):
        pl.semaphore_signal(
            barrier, inc=1, device_id=(lax.rem(high + i, half) * 2 + core, me), device_id_type=MESH
        )
    pl.semaphore_signal(barrier, inc=1, device_id=(peer, me), device_id_type=MESH)

    own_green = pltpu.make_async_copy(green_hbm.at[0], green.at[shot], green_sem)
    own_green.start()
    for x in order[2:] + order[:2]:
        prev_copy(x).start()
        diag_copy(x).start()
        cross_copy(x).start()

    for field in (ua, ub):
        field[0] = jnp.zeros(field.shape[1:], F32)
        field[cx + 1] = jnp.zeros(field.shape[1:], F32)
        for x in range(cx):
            field[1 + x, pl.ds(0, PAD)] = jnp.zeros((PAD, nz), F32)
            field[1 + x, pl.ds(PAD + ny, PAD)] = jnp.zeros((PAD, nz), F32)

    pl.semaphore_wait(barrier, n - 1 + half)

    def green_copy(i):
        return pltpu.make_async_remote_copy(
            src_ref=green_hbm.at[0],
            dst_ref=green.at[shot],
            send_sem=green_send.at[i],
            recv_sem=green_recv.at[i],
            device_id=(lax.rem(high + i, half) * 2 + core, me) if i else (peer, me),
            device_id_type=MESH,
        )

    def green_wait(i):
        source = lax.rem(high - i + half, half) * 2 + core if i else peer
        pltpu.make_async_remote_copy(
            src_ref=green_hbm.at[0],
            dst_ref=green.at[source],
            send_sem=green_send.at[i],
            recv_sem=green_recv.at[i],
            device_id=(peer, me),
            device_id_type=MESH,
        ).wait_recv()

    def pass_copy(i, which):
        slot = lax.rem(high - i + half, half) * 2 + which
        return pltpu.make_async_remote_copy(
            src_ref=green.at[slot],
            dst_ref=green.at[slot],
            send_sem=pass_send.at[i],
            recv_sem=pass_recv.at[i],
            device_id=(peer, me),
            device_id_type=MESH,
        )

    for i in list(range(1, half)) + [0]:
        green_copy(i).start()

    def edge_copy(t, side, k):
        rows = pl.ds(k * chunk, chunk)
        return pltpu.make_async_remote_copy(
            src_ref=send_edge.at[t, side, rows],
            dst_ref=recv_edge.at[t, side, rows],
            send_sem=edge_send.at[t, side, k],
            recv_sem=edge_recv.at[t, side, k],
            device_id=(shot, lax.rem(me + 1 - 2 * side + n, n)),
            device_id_type=MESH,
        )

    def sends_to(side):
        return me < n - 1 if side == 0 else me > 0

    def hears_from(side):
        return me > 0 if side == 0 else me < n - 1

    def send_edges(field, t, k):
        for side in (0, 1):
            plane = cx if side == 0 else 1
            send_edge[t, side, pl.ds(k * chunk, chunk)] = field[
                plane, pl.ds(PAD + k * chunk, chunk)
            ].astype(BF16)

            @pl.when(sends_to(side))
            def _():
                edge_copy(t, side, k).start()

    def take_edges(field, t, k):
        for side in (0, 1):
            plane = 0 if side == 0 else cx + 1

            @pl.when(hears_from(side))
            def _():
                edge_copy(t, side, k).wait_recv()
                field[plane, pl.ds(PAD + k * chunk, chunk)] = recv_edge[
                    t, side, pl.ds(k * chunk, chunk)
                ].astype(F32)

    now_copy(0).wait()
    now_copy(cx - 1).wait()
    for k in range(CHUNKS):
        send_edges(ub, 0, k)

    for copy in small:
        copy.wait()
    cells = rec_cell[...]
    row_col = column_of((cells // nz).astype(F32))
    lane_col = column_of((cells % nz).astype(F32))
    rec_rows[...] = jnp.where(
        lax.broadcasted_iota(jnp.int32, (points, cx * ny), 1).astype(F32) == row_col, 1.0, 0.0
    ).astype(BF16)
    lanes = lax.broadcasted_iota(jnp.int32, (points, nz), 1).astype(F32)
    rec_lanes[...] = jnp.where(lanes == lane_col, 1.0, 0.0)
    cells = emit_cell[...]
    hits = jnp.where(
        lax.broadcasted_iota(jnp.int32, (cx * ny, points), 0) == cells // nz, 1.0, 0.0
    ).astype(BF16)
    emit_rows[:, pl.ds(0, points)] = hits
    emit_rows[:, pl.ds(points, points)] = hits
    emit_lanes[...] = jnp.where(lanes == column_of((cells % nz).astype(F32)), 1.0, 0.0)
    series[...] = jnp.zeros(series.shape, F32)
    series[pl.ds(0, hist), :] = past[...].astype(F32).reshape(hist, points)

    def record(field, t):
        picked = jnp.zeros((points, nz), F32)
        for x in range(cx):
            picked = picked + jnp.dot(
                rec_rows[:, pl.ds(x * ny, ny)],
                field[1 + x, inner].astype(BF16),
                preferred_element_type=F32,
            )
        sample = row_of(jnp.sum(picked * rec_lanes[...], axis=1, keepdims=True))
        recorded[pl.ds(t, 1), :] = sample
        series[pl.ds(hist + t, 1), :] = sample

    def sum_copy(t, i):
        to = lax.rem(me + i, n)
        return pltpu.make_async_remote_copy(
            src_ref=send_sum.at[t, to],
            dst_ref=recv_sum.at[t, me],
            send_sem=sum_send.at[t, i - 1],
            recv_sem=sum_recv.at[t, i - 1],
            device_id=(shot, to),
            device_id_type=MESH,
        )

    def sum_wait(t, i):
        pltpu.make_async_remote_copy(
            src_ref=send_sum.at[t, lax.rem(me + i, n)],
            dst_ref=recv_sum.at[t, lax.rem(me - i + n, n)],
            send_sem=sum_send.at[t, i - 1],
            recv_sem=sum_recv.at[t, i - 1],
            device_id=(shot, lax.rem(me + i, n)),
            device_id_type=MESH,
        ).wait_recv()

    def emit_start(t):
        total = None
        steps_of = lax.broadcasted_iota(jnp.int32, series.shape, 0)
        for lag in range(shots):
            where_at = hist + t - delays[lag]
            chosen = jnp.sum(jnp.where(steps_of == where_at, series[...], 0.0), axis=0, keepdims=True)
            part = lax.dot_general(
                jnp.broadcast_to(chosen, (16, points)).astype(BF16),
                green[lag],
                (((1,), (1,)), ((), ())),
                preferred_element_type=F32,
            )
            total = part if total is None else total + part
        for k in range(n):
            send_sum[t, k] = total[0:1, k * points:(k + 1) * points]
        for i in range(1, n):
            sum_copy(t, i).start()
        recv_sum[t, me] = send_sum[t, me]

    def emit_finish(t):
        for i in range(1, n):
            sum_wait(t, i)
        total = recv_sum[t, 0]
        for k in range(1, n):
            total = total + recv_sum[t, k]
        spread = emit_lanes[...] * column_of(total)
        upper = spread.astype(BF16)
        weights[pl.ds(0, points), :] = upper
        weights[pl.ds(points, points), :] = (spread - upper.astype(F32)).astype(BF16)

    def emission_on(x):
        return jnp.dot(
            emit_rows[pl.ds(x * ny, ny), :], weights[...], preferred_element_type=F32
        )

    lane = lax.broadcasted_iota(jnp.int32, (ROWS, nz), 1)
    not_first = lane > 0
    not_last = lane < nz - 1

    def ahead(v):
        return jnp.where(not_last, pltpu.roll(v, nz - 1, 1), 0.0)

    def behind(v):
        return jnp.where(not_first, pltpu.roll(v, 1, 1), 0.0)

    def later(slab):
        return pltpu.roll(slab, ROWS + 2 * PAD - 1, 0)[PAD:PAD + ROWS]

    def sooner(slab):
        return pltpu.roll(slab, 1, 0)[PAD:PAD + ROWS]

    def advance(earlier, current, x, start, rows):
        def body(i, _):
            y = pl.multiple_of(start + i * ROWS, ROWS)
            here = pl.ds(pl.multiple_of(y + PAD, PAD), ROWS)
            around = pl.ds(y, ROWS + 2 * PAD)
            at = pl.ds(y, ROWS)
            centre = current[1 + x, around]
            difference = current[2 + x, around] - current[x, around]
            u = current[1 + x, here]
            above, below = current[2 + x, here], current[x, here]
            u_up, u_down = later(centre), sooner(centre)
            twice = 2.0 * u
            second = diag[0, x, at] * (above + below - twice)
            second = second + diag[1, x, at] * (u_up + u_down - twice)
            second = second + diag[2, x, at] * (ahead(u) + behind(u) - twice)
            across = above - below
            slope = u_up - u_down
            mixed = cross[0, x, at] * (
                later(difference) - sooner(difference)
            )
            mixed = mixed + cross[1, x, at] * (ahead(across) - behind(across))
            mixed = mixed + cross[2, x, at] * (ahead(slope) - behind(slope))
            earlier[1 + x, here] = twice - earlier[1 + x, here] + second + 0.5 * mixed
            return 0

        lax.fori_loop(0, rows // ROWS, body, 0, unroll=2)

    for x in range(1, cx - 1):
        now_copy(x).wait()

    for t in range(STEPS):
        earlier, current = (ua, ub) if t % 2 == 0 else (ub, ua)
        record(current, t)
        if t > 0:
            emit_start(t)
        for x in range(1, cx - 1):
            if t == 0:
                prev_copy(x).wait()
                diag_copy(x).wait()
                cross_copy(x).wait()
            advance(earlier, current, x, 0, ny)
        if t == 0:
            for i in range(1, half):
                green_wait(i)
                pass_copy(i, core).start()
            own_green.wait()
            green_wait(0)
            for i in range(1, half):
                pass_copy(i, 1 - core).wait_recv()
            emit_start(t)
            for x in (0, cx - 1):
                prev_copy(x).wait()
                diag_copy(x).wait()
                cross_copy(x).wait()
        emit_finish(t)
        for x in range(1, cx - 1):
            earlier[1 + x, inner] += emission_on(x)
        for x in (0, cx - 1):
            earlier[1 + x, inner] -= emission_on(x)
        take_edges(current, t, 0)
        for k in range(CHUNKS):
            if k + 1 < CHUNKS:
                take_edges(current, t, k + 1)
            for x in (0, cx - 1):
                advance(earlier, current, x, k * chunk, chunk)
            if t + 1 < STEPS:
                send_edges(earlier, t + 1, k)
        if t == STEPS - 2:
            before = pltpu.make_async_copy(
                earlier.at[pl.ds(1, cx), inner], before_hbm.at[0], out_sem.at[0]
            )
            before.start()
        if t == STEPS - 1:
            after = pltpu.make_async_copy(
                earlier.at[pl.ds(1, cx), inner], after_hbm.at[0], out_sem.at[1]
            )
            after.start()

    for i in range(half):
        green_copy(i).wait_send()
    for i in range(1, half):
        pass_copy(i, core).wait_send()
    for t in range(STEPS):
        for i in range(1, n):
            sum_copy(t, i).wait_send()
        for side in (0, 1):

            @pl.when(sends_to(side))
            def _():
                for k in range(CHUNKS):
                    edge_copy(t, side, k).wait_send()

    before.wait()
    after.wait()


def on_device(
    n, shots, field_prev, field_now, diag_coef, cross_coef, green, delays, past, rec_cell, emit_cell
):
    _, cx, ny, nz = field_prev.shape
    hist, _, points = past.shape
    _, emits, _ = green.shape
    half = shots // 2
    vmem = pl.BlockSpec(memory_space=pltpu.VMEM)
    hbm = pl.BlockSpec(memory_space=pl.ANY)
    dma = pltpu.SemaphoreType.DMA
    depth = -(-(hist + STEPS) // 8) * 8
    before, after, recorded = pl.pallas_call(
        functools.partial(kernel, n, shots),
        out_shape=(
            jax.ShapeDtypeStruct(field_prev.shape, F32),
            jax.ShapeDtypeStruct(field_prev.shape, F32),
            jax.ShapeDtypeStruct((STEPS, points), F32),
        ),
        in_specs=[hbm] * 5 + [pl.BlockSpec(memory_space=pltpu.SMEM)] + [hbm] * 3,
        out_specs=(hbm, hbm, vmem),
        scratch_shapes=[
            pltpu.VMEM(past.shape, BF16),
            pltpu.VMEM(rec_cell.shape, jnp.int32),
            pltpu.VMEM(emit_cell.shape, jnp.int32),
            pltpu.VMEM((cx + 2, ny + 2 * PAD, nz), F32),
            pltpu.VMEM((cx + 2, ny + 2 * PAD, nz), F32),
            pltpu.VMEM((3, cx, ny, nz), F32),
            pltpu.VMEM((3, cx, ny, nz), F32),
            pltpu.VMEM((shots, emits, points), BF16),
            pltpu.VMEM((depth, points), F32),
            pltpu.VMEM((STEPS, 2, ny, nz), BF16),
            pltpu.VMEM((STEPS, 2, ny, nz), BF16),
            pltpu.VMEM((STEPS, n, 1, points), F32),
            pltpu.VMEM((STEPS, n, 1, points), F32),
            pltpu.VMEM((points, cx * ny), BF16),
            pltpu.VMEM((points, nz), F32),
            pltpu.VMEM((cx * ny, 2 * points), BF16),
            pltpu.VMEM((points, nz), F32),
            pltpu.VMEM((2 * points, nz), BF16),
            dma((3,)),
            dma((cx,)),
            dma((cx,)),
            dma((2, cx)),
            dma,
            dma((half,)),
            dma((half,)),
            dma((half,)),
            dma((half,)),
            dma((STEPS, 2, CHUNKS)),
            dma((STEPS, 2, CHUNKS)),
            dma((STEPS, n - 1)),
            dma((STEPS, n - 1)),
            dma((2,)),
        ],
        compiler_params=pltpu.CompilerParams(
            collective_id=0, has_side_effects=True, vmem_limit_bytes=62 * 1024 * 1024
        ),
    )(
        field_prev,
        field_now,
        diag_coef,
        cross_coef,
        green,
        delays,
        past,
        rec_cell,
        emit_cell,
    )
    return before, after, recorded.astype(BF16).reshape(STEPS, 1, points)


def solution(mesh):
    return jax.shard_map(
        functools.partial(on_device, mesh.shape["brick"], mesh.shape["shot"]),
        mesh=mesh,
        in_specs=(
            P("shot", "brick", None, None),
            P("shot", "brick", None, None),
            P(None, "brick", None, None),
            P(None, "brick", None, None),
            P("shot", None, "brick"),
            P(),
            P(None, "shot", "brick"),
            P("shot", "brick"),
            P("shot", "brick"),
        ),
        out_specs=(
            P("shot", "brick", None, None),
            P("shot", "brick", None, None),
            P(None, "shot", "brick"),
        ),
        check_vma=False,
    )
```

```python
import functools

import jax
import jax.numpy as jnp
from jax import lax
from jax.experimental import pallas as pl
from jax.experimental.pallas import tpu as pltpu
from jax.sharding import PartitionSpec as P

STEPS = 3
MESH = pl.DeviceIdType.MESH
PAD = 8
ROWS = 32
CHUNKS = 4
F32 = jnp.float32
BF16 = jnp.bfloat16


def column_of(row):
    k = row.shape[1]
    eye = lax.broadcasted_iota(jnp.int32, (k, k), 0) == lax.broadcasted_iota(jnp.int32, (k, k), 1)
    return jnp.sum(jnp.where(eye, jnp.broadcast_to(row, (k, k)), 0.0), axis=1, keepdims=True)


def row_of(col):
    k = col.shape[0]
    eye = lax.broadcasted_iota(jnp.int32, (k, k), 0) == lax.broadcasted_iota(jnp.int32, (k, k), 1)
    return jnp.sum(jnp.where(eye, jnp.broadcast_to(col, (k, k)), 0.0), axis=0, keepdims=True)


def kernel(
    n, shots, prev_hbm, now_hbm, diag_hbm, cross_hbm, green_hbm, delays, past_hbm, rec_hbm, emit_hbm,
    before_hbm, after_hbm, recorded,
    past, rec_cell, emit_cell, ua, ub, diag, cross, green, series, send_edge, recv_edge, send_sum, recv_sum,
    rec_rows, rec_lanes, emit_rows, emit_lanes, weights,
    small_sem, now_sem, prev_sem, coef_sem, green_sem, green_send, green_recv, pass_send, pass_recv,
    edge_send, edge_recv, sum_send, sum_recv, out_sem,
):
    me = lax.axis_index("brick")
    shot = lax.axis_index("shot")
    cx, ny, nz = prev_hbm.shape[1:]
    hist = past.shape[0]
    points = rec_cell.shape[1]
    chunk = ny // CHUNKS
    half = shots // 2
    core = lax.rem(shot, 2)
    high = shot // 2
    peer = shot + 1 - 2 * core
    inner = pl.ds(PAD, ny)

    order = [0, cx - 1] + list(range(1, cx - 1))

    def now_copy(x):
        return pltpu.make_async_copy(now_hbm.at[0, x], ub.at[1 + x, inner], now_sem.at[x])

    def prev_copy(x):
        return pltpu.make_async_copy(prev_hbm.at[0, x], ua.at[1 + x, inner], prev_sem.at[x])

    def diag_copy(x):
        return pltpu.make_async_copy(diag_hbm.at[:, x], diag.at[:, x], coef_sem.at[0, x])

    def cross_copy(x):
        return pltpu.make_async_copy(cross_hbm.at[:, x], cross.at[:, x], coef_sem.at[1, x])

    for x in order:
        now_copy(x).start()
    small = [
        pltpu.make_async_copy(source, target, small_sem.at[i])
        for i, (source, target) in enumerate(
            ((past_hbm, past), (rec_hbm, rec_cell), (emit_hbm, emit_cell))
        )
    ]
    for copy in small:
        copy.start()

    barrier = pltpu.get_barrier_semaphore()
    for i in range(1, n):
        pl.semaphore_signal(
            barrier, inc=1, device_id=(shot, lax.rem(me + i, n)), device_id_type=MESH
        )
    for i in range(1, half):
        pl.semaphore_signal(
            barrier, inc=1, device_id=(lax.rem(high + i, half) * 2 + core, me), device_id_type=MESH
        )
    pl.semaphore_signal(barrier, inc=1, device_id=(peer, me), device_id_type=MESH)

    own_green = pltpu.make_async_copy(green_hbm.at[0], green.at[shot], green_sem)
    own_green.start()
    for x in order[2:] + order[:2]:
        prev_copy(x).start()
        diag_copy(x).start()
        cross_copy(x).start()

    for field in (ua, ub):
        field[0] = jnp.zeros(field.shape[1:], F32)
        field[cx + 1] = jnp.zeros(field.shape[1:], F32)
        for x in range(cx):
            field[1 + x, pl.ds(0, PAD)] = jnp.zeros((PAD, nz), F32)
            field[1 + x, pl.ds(PAD + ny, PAD)] = jnp.zeros((PAD, nz), F32)

    pl.semaphore_wait(barrier, n - 1 + half)

    def green_copy(i):
        return pltpu.make_async_remote_copy(
            src_ref=green_hbm.at[0],
            dst_ref=green.at[shot],
            send_sem=green_send.at[i],
            recv_sem=green_recv.at[i],
            device_id=(lax.rem(high + i, half) * 2 + core, me) if i else (peer, me),
            device_id_type=MESH,
        )

    def green_wait(i):
        source = lax.rem(high - i + half, half) * 2 + core if i else peer
        pltpu.make_async_remote_copy(
            src_ref=green_hbm.at[0],
            dst_ref=green.at[source],
            send_sem=green_send.at[i],
            recv_sem=green_recv.at[i],
            device_id=(peer, me),
            device_id_type=MESH,
        ).wait_recv()

    def pass_copy(i, which):
        slot = lax.rem(high - i + half, half) * 2 + which
        return pltpu.make_async_remote_copy(
            src_ref=green.at[slot],
            dst_ref=green.at[slot],
            send_sem=pass_send.at[i],
            recv_sem=pass_recv.at[i],
            device_id=(peer, me),
            device_id_type=MESH,
        )

    for i in list(range(1, half)) + [0]:
        green_copy(i).start()

    def edge_copy(t, side, k):
        rows = pl.ds(k * chunk, chunk)
        return pltpu.make_async_remote_copy(
            src_ref=send_edge.at[t, side, rows],
            dst_ref=recv_edge.at[t, side, rows],
            send_sem=edge_send.at[t, side, k],
            recv_sem=edge_recv.at[t, side, k],
            device_id=(shot, lax.rem(me + 1 - 2 * side + n, n)),
            device_id_type=MESH,
        )

    def sends_to(side):
        return me < n - 1 if side == 0 else me > 0

    def hears_from(side):
        return me > 0 if side == 0 else me < n - 1

    def send_edges(field, t, side):
        send_edge[t, side] = field[cx if side == 0 else 1, inner].astype(BF16)

        @pl.when(sends_to(side))
        def _():
            for k in range(CHUNKS):
                edge_copy(t, side, k).start()

    def take_edges(field, t, k):
        for side in (0, 1):
            plane = 0 if side == 0 else cx + 1

            @pl.when(hears_from(side))
            def _():
                edge_copy(t, side, k).wait_recv()
                field[plane, pl.ds(PAD + k * chunk, chunk)] = recv_edge[
                    t, side, pl.ds(k * chunk, chunk)
                ].astype(F32)

    now_copy(0).wait()
    send_edges(ub, 0, 1)
    now_copy(cx - 1).wait()
    send_edges(ub, 0, 0)

    for copy in small:
        copy.wait()
    cells = rec_cell[...]
    row_col = column_of((cells // nz).astype(F32))
    lane_col = column_of((cells % nz).astype(F32))
    rec_rows[...] = jnp.where(
        lax.broadcasted_iota(jnp.int32, (points, cx * ny), 1).astype(F32) == row_col, 1.0, 0.0
    ).astype(BF16)
    lanes = lax.broadcasted_iota(jnp.int32, (points, nz), 1).astype(F32)
    rec_lanes[...] = jnp.where(lanes == lane_col, 1.0, 0.0)
    cells = emit_cell[...]
    hits = jnp.where(
        lax.broadcasted_iota(jnp.int32, (cx * ny, points), 0) == cells // nz, 1.0, 0.0
    ).astype(BF16)
    emit_rows[:, pl.ds(0, points)] = hits
    emit_rows[:, pl.ds(points, points)] = hits
    emit_lanes[...] = jnp.where(lanes == column_of((cells % nz).astype(F32)), 1.0, 0.0)
    series[...] = jnp.zeros(series.shape, F32)
    series[pl.ds(0, hist), :] = past[...]

    def record(field, t):
        picked = jnp.zeros((points, nz), F32)
        for x in range(cx):
            picked = picked + jnp.dot(
                rec_rows[:, pl.ds(x * ny, ny)],
                field[1 + x, inner].astype(BF16),
                preferred_element_type=F32,
            )
        sample = row_of(jnp.sum(picked * rec_lanes[...], axis=1, keepdims=True))
        recorded[pl.ds(t, 1), :] = sample
        series[pl.ds(hist + t, 1), :] = sample

    def sum_copy(t, i):
        to = lax.rem(me + i, n)
        return pltpu.make_async_remote_copy(
            src_ref=send_sum.at[t, to],
            dst_ref=recv_sum.at[t, me],
            send_sem=sum_send.at[t, i - 1],
            recv_sem=sum_recv.at[t, i - 1],
            device_id=(shot, to),
            device_id_type=MESH,
        )

    def sum_wait(t, i):
        pltpu.make_async_remote_copy(
            src_ref=send_sum.at[t, lax.rem(me + i, n)],
            dst_ref=recv_sum.at[t, lax.rem(me - i + n, n)],
            send_sem=sum_send.at[t, i - 1],
            recv_sem=sum_recv.at[t, i - 1],
            device_id=(shot, lax.rem(me + i, n)),
            device_id_type=MESH,
        ).wait_recv()

    def emit_start(t):
        total = None
        steps_of = lax.broadcasted_iota(jnp.int32, series.shape, 0)
        for lag in range(shots):
            where_at = hist + t - delays[lag]
            chosen = jnp.sum(jnp.where(steps_of == where_at, series[...], 0.0), axis=0, keepdims=True)
            part = lax.dot_general(
                jnp.broadcast_to(chosen, (16, points)).astype(BF16),
                green[lag],
                (((1,), (1,)), ((), ())),
                preferred_element_type=F32,
            )
            total = part if total is None else total + part
        for k in range(n):
            send_sum[t, k] = total[0:1, k * points:(k + 1) * points]
        for i in range(1, n):
            sum_copy(t, i).start()
        recv_sum[t, me] = send_sum[t, me]

    def emit_finish(t):
        for i in range(1, n):
            sum_wait(t, i)
        total = recv_sum[t, 0]
        for k in range(1, n):
            total = total + recv_sum[t, k]
        spread = emit_lanes[...] * column_of(total)
        upper = spread.astype(BF16)
        weights[pl.ds(0, points), :] = upper
        weights[pl.ds(points, points), :] = (spread - upper.astype(F32)).astype(BF16)

    def emission_on(x):
        return jnp.dot(
            emit_rows[pl.ds(x * ny, ny), :], weights[...], preferred_element_type=F32
        )

    lane = lax.broadcasted_iota(jnp.int32, (ROWS, nz), 1)
    not_first = lane > 0
    not_last = lane < nz - 1

    def ahead(v):
        return jnp.where(not_last, pltpu.roll(v, nz - 1, 1), 0.0)

    def behind(v):
        return jnp.where(not_first, pltpu.roll(v, 1, 1), 0.0)

    def later(slab):
        return pltpu.roll(slab, ROWS + 2 * PAD - 1, 0)[PAD:PAD + ROWS]

    def sooner(slab):
        return pltpu.roll(slab, 1, 0)[PAD:PAD + ROWS]

    def advance(earlier, current, x, start, rows):
        def body(i, _):
            y = pl.multiple_of(start + i * ROWS, ROWS)
            here = pl.ds(pl.multiple_of(y + PAD, PAD), ROWS)
            around = pl.ds(y, ROWS + 2 * PAD)
            at = pl.ds(y, ROWS)
            centre = current[1 + x, around]
            difference = current[2 + x, around] - current[x, around]
            u = current[1 + x, here]
            above, below = current[2 + x, here], current[x, here]
            u_up, u_down = later(centre), sooner(centre)
            twice = 2.0 * u
            second = diag[0, x, at] * (above + below - twice)
            second = second + diag[1, x, at] * (u_up + u_down - twice)
            second = second + diag[2, x, at] * (ahead(u) + behind(u) - twice)
            across = above - below
            slope = u_up - u_down
            mixed = cross[0, x, at] * (
                later(difference) - sooner(difference)
            )
            mixed = mixed + cross[1, x, at] * (ahead(across) - behind(across))
            mixed = mixed + cross[2, x, at] * (ahead(slope) - behind(slope))
            earlier[1 + x, here] = twice - earlier[1 + x, here] + second + 0.5 * mixed
            return 0

        lax.fori_loop(0, rows // ROWS, body, 0, unroll=2)

    for x in range(1, cx - 1):
        now_copy(x).wait()

    for t in range(STEPS):
        earlier, current = (ua, ub) if t % 2 == 0 else (ub, ua)
        record(current, t)
        if t > 0:
            emit_start(t)
        for x in range(1, cx - 1):
            if t == 0:
                prev_copy(x).wait()
                diag_copy(x).wait()
                cross_copy(x).wait()
            advance(earlier, current, x, 0, ny)
        if t == 0:
            for i in range(1, half):
                green_wait(i)
                pass_copy(i, core).start()
            for x in (0, cx - 1):
                prev_copy(x).wait()
                diag_copy(x).wait()
                cross_copy(x).wait()
        take_edges(current, t, 0)
        for k in range(CHUNKS):
            if k + 1 < CHUNKS:
                take_edges(current, t, k + 1)
            for x in (0, cx - 1):
                advance(earlier, current, x, k * chunk, chunk)
        if t == 0:
            own_green.wait()
            green_wait(0)
            for i in range(1, half):
                pass_copy(i, 1 - core).wait_recv()
            emit_start(t)
        emit_finish(t)
        for side, x in ((0, cx - 1), (1, 0)):
            earlier[1 + x, inner] += emission_on(x)
            if t + 1 < STEPS:
                send_edges(earlier, t + 1, side)
        for x in range(1, cx - 1):
            earlier[1 + x, inner] += emission_on(x)
        if t == STEPS - 2:
            before = pltpu.make_async_copy(
                earlier.at[pl.ds(1, cx), inner], before_hbm.at[0], out_sem.at[0]
            )
            before.start()
        if t == STEPS - 1:
            after = pltpu.make_async_copy(
                earlier.at[pl.ds(1, cx), inner], after_hbm.at[0], out_sem.at[1]
            )
            after.start()

    for i in range(half):
        green_copy(i).wait_send()
    for i in range(1, half):
        pass_copy(i, core).wait_send()
    for t in range(STEPS):
        for i in range(1, n):
            sum_copy(t, i).wait_send()
        for side in (0, 1):

            @pl.when(sends_to(side))
            def _():
                for k in range(CHUNKS):
                    edge_copy(t, side, k).wait_send()

    before.wait()
    after.wait()


def on_device(
    n, shots, field_prev, field_now, diag_coef, cross_coef, green, delays, past, rec_cell, emit_cell
):
    _, cx, ny, nz = field_prev.shape
    hist, _, points = past.shape
    _, emits, _ = green.shape
    half = shots // 2
    vmem = pl.BlockSpec(memory_space=pltpu.VMEM)
    hbm = pl.BlockSpec(memory_space=pl.ANY)
    fixed = pl.BlockSpec(memory_space=pltpu.HBM)
    dma = pltpu.SemaphoreType.DMA
    depth = -(-(hist + STEPS) // 8) * 8
    before, after, recorded = pl.pallas_call(
        functools.partial(kernel, n, shots),
        out_shape=(
            jax.ShapeDtypeStruct(field_prev.shape, F32),
            jax.ShapeDtypeStruct(field_prev.shape, F32),
            jax.ShapeDtypeStruct((STEPS, points), F32),
        ),
        in_specs=[fixed] * 5 + [pl.BlockSpec(memory_space=pltpu.SMEM)] + [fixed] * 3,
        out_specs=(hbm, hbm, vmem),
        scratch_shapes=[
            pltpu.VMEM((hist, points), F32),
            pltpu.VMEM(rec_cell.shape, jnp.int32),
            pltpu.VMEM(emit_cell.shape, jnp.int32),
            pltpu.VMEM((cx + 2, ny + 2 * PAD, nz), F32),
            pltpu.VMEM((cx + 2, ny + 2 * PAD, nz), F32),
            pltpu.VMEM((3, cx, ny, nz), F32),
            pltpu.VMEM((3, cx, ny, nz), F32),
            pltpu.VMEM((shots, emits, points), BF16),
            pltpu.VMEM((depth, points), F32),
            pltpu.VMEM((STEPS, 2, ny, nz), BF16),
            pltpu.VMEM((STEPS, 2, ny, nz), BF16),
            pltpu.VMEM((STEPS, n, 1, points), F32),
            pltpu.VMEM((STEPS, n, 1, points), F32),
            pltpu.VMEM((points, cx * ny), BF16),
            pltpu.VMEM((points, nz), F32),
            pltpu.VMEM((cx * ny, 2 * points), BF16),
            pltpu.VMEM((points, nz), F32),
            pltpu.VMEM((2 * points, nz), BF16),
            dma((3,)),
            dma((cx,)),
            dma((cx,)),
            dma((2, cx)),
            dma,
            dma((half,)),
            dma((half,)),
            dma((half,)),
            dma((half,)),
            dma((STEPS, 2, CHUNKS)),
            dma((STEPS, 2, CHUNKS)),
            dma((STEPS, n - 1)),
            dma((STEPS, n - 1)),
            dma((2,)),
        ],
        compiler_params=pltpu.CompilerParams(
            collective_id=0, has_side_effects=True, vmem_limit_bytes=48 * 1024 * 1024
        ),
    )(
        field_prev,
        field_now,
        diag_coef,
        cross_coef,
        green,
        delays,
        past.reshape(hist, points).astype(F32),
        rec_cell,
        emit_cell,
    )
    return before, after, recorded.astype(BF16).reshape(STEPS, 1, points)


def solution(mesh):
    return jax.shard_map(
        functools.partial(on_device, mesh.shape["brick"], mesh.shape["shot"]),
        mesh=mesh,
        in_specs=(
            P("shot", "brick", None, None),
            P("shot", "brick", None, None),
            P(None, "brick", None, None),
            P(None, "brick", None, None),
            P("shot", None, "brick"),
            P(),
            P(None, "shot", "brick"),
            P("shot", "brick"),
            P("shot", "brick"),
        ),
        out_specs=(
            P("shot", "brick", None, None),
            P("shot", "brick", None, None),
            P(None, "shot", "brick"),
        ),
        check_vma=False,
    )
```
